32 devices in a mesh: dp: 16 (over z, y, x), tensor: 2 (over core).
Axes of the slice: x: 2, y: 2, z: 4, core: 2. Of those that a mesh axis runs over, the one named last changes fastest.
Arguments:
- query_in: bfloat16 [24576, 4096], P('dp', 'tensor'), may hold values from -6 to 6
- key_in: bfloat16 [24576, 4096], P('dp', 'tensor'), may hold values from -6 to 6
- value_in: bfloat16 [24576, 4096], P('dp', 'tensor'), may hold values from -6 to 6
- feat_filter: float32 [3, 7, 4096], P(None, None, 'tensor'), may hold values from -2.5 to 2.5
- inner_filter: float32 [7, 4096], P(None, 'tensor'), may hold values from -2.5 to 2.5
- out_weight: bfloat16 [4096, 4096], P('tensor'), may hold values from -0.125 to 0.125
- doc_pos: int32 [24576], P('dp'), may hold values from 0 to 511, as said below
- counts: int32 [16], P('dp'), may hold values from 1 to 12, 184 in all
- destination: int32 [192, 1], P('dp'), may hold values from 0 to 15; in each aligned block of 12 rows (0 to 11, 12 to 23, ...) no two rows name the same one
Outputs:
- routed: bfloat16 [32768, 4096], P('dp', 'tensor')
The draws below stay inside these ranges and needn't reach their ends.
Inputs may be any that keep to these rules, and one draw needn't show every extreme that they name: `doc_pos`: 0 at the first row of a document (row 0 and every multiple of 512 are such rows), else one more than on the row before; rows 0 to 511 form one document. `counts`: one device has all its blocks filled. Among the 12 entries of one dp device no destination appears twice.
All inputs are finite; a program needn't handle non-finite values.
Results may differ from the reference program's by a relative error of at most 0.0058.
Values may be sent and summed in bfloat16 or wider, within the bound.
No kernel may reach another device: no remote copies, remote signals or barrier semaphores. Data moves between devices by JAX's collectives and lax.ppermute only.
A program may use at most 128 MiB of HBM per device.

```python
import math
import jax
import jax.numpy as jnp
import numpy as np
from jax import lax

BLK = 128
NBLK = 12
CHAN = 4096
OUTW = 4096
TAPS = 7
TOKENS = 24576
N_DP = 16
N_TENSOR = 2


def draw_doc_pos(key, part):
    row_index = jnp.arange(TOKENS, dtype=jnp.int32)
    marks = jax.random.randint(key, (TOKENS,), 0, 3 * BLK)
    marks = jnp.where(row_index < 4 * BLK, 1, marks)
    is_start = (marks == 0) | (row_index % (4 * BLK) == 0)
    starts = jnp.where(is_start, row_index, 0).astype(jnp.int32)
    return (row_index - lax.cummax(starts, axis=0)).astype(jnp.int32)


def strengthened(entries, key, source, target, blocks, factor):
    owner, partner = [(jnp.arange(entries.shape[axis_at]) // (entries.shape[axis_at] // blocks)).reshape([-1 if axis == axis_at else 1 for axis in range(entries.ndim)]) for axis_at in (source, target)]
    chosen = jax.random.permutation(key, blocks)[partner]
    strong = (owner == chosen) | (owner == (partner + blocks // 2) % blocks)
    return jnp.where(strong, factor * entries, entries)


def levels(key, dims, split, least, top_value):
    def one(axis_at, shards_of):
        draws = jax.random.uniform(jax.random.fold_in(jax.random.fold_in(key, 6), axis_at), (shards_of,), jnp.float32, least / len(split), top_value / len(split))
        return jnp.repeat(jnp.exp(draws), dims[axis_at] // shards_of).reshape((-1,) + (1,) * (len(dims) - axis_at - 1))

    gain = one(*split[0])
    for cut in split[1:]:
        gain = gain * one(*cut)
    return gain


def split_up(number_of, total, limit, skew):
    weights = [(1 << 20) // math.isqrt(rank ** skew) + 1 for rank in range(2, number_of + 1)]
    rest, given = total - limit - (number_of - 1), [1] * (number_of - 1)
    while rest > 0:
        movable = [i for i in range(number_of - 1) if given[i] < limit]
        mass, left = sum([weights[i] for i in movable]), rest
        for i in movable:
            extra = min(limit - given[i], max(1, left * weights[i] // mass), rest)
            given[i] = given[i] + extra
            rest = rest - extra
    return np.array([limit] + given)


def uneven_parts(own_key, amount, total, reach, lean):
    if amount == 2:
        one = jax.random.randint(own_key, (), max(1, total - reach), min(reach, total - 1) + 1)
        return jnp.stack([one, total - one])
    lengths = jnp.asarray(split_up(amount, total, reach, lean), jnp.int32)
    couples = (amount - 1) // 2
    donor, receiver = lengths[1:1 + 2 * couples:2], lengths[2:2 + 2 * couples:2]
    slack = jnp.minimum(donor - 1, reach - receiver)
    moved = jax.random.randint(jax.random.fold_in(own_key, 1), (couples,), 0, 1 << 20) % (slack + 1)
    lengths = lengths.at[1:1 + 2 * couples:2].set(donor - moved).at[2:2 + 2 * couples:2].set(receiver + moved)
    return lengths[jax.random.permutation(jax.random.fold_in(own_key, 2), amount)]


def shared_out(rng, own, number, rows, count, top, bound, skew):
    order = jax.random.permutation(rng, count)
    heavy_load, usual = shares(count, rows * top, bound, skew, True), shares(count, rows * top, bound, skew, False)
    places = jnp.arange(count)

    def named(tallies, turn):
        used = int((tallies > 0).sum())
        fixed = max(1, used // 4)
        moved = fixed + (places - fixed + turn * (used - fixed)) % max(1, count - fixed)
        return jnp.zeros((count,), jnp.int32).at[order[jnp.where(places < fixed, places, moved)]].set(jnp.asarray(tallies, jnp.int32))

    tallies = jnp.where(number % 4 == 0, named(heavy_load, number // 4), named(usual, number - number // 4 - 1))
    mixed = jax.random.permutation(jax.random.fold_in(own, 3), count)
    giver, taker = mixed[0:count // 2 * 2:2], mixed[1:count // 2 * 2:2]
    room = jnp.minimum(tallies[giver] - 1, bound - tallies[taker]) // 2
    room = jnp.where((giver == order[0]) | (taker == order[0]) | (tallies[taker] == 0), 0, jnp.maximum(room, 0))
    moved = jax.random.randint(jax.random.fold_in(own, 4), (count // 2,), 0, 1 << 20) % (room + 1)
    tallies = tallies.at[giver].add(-moved).at[taker].add(moved)
    members = jnp.searchsorted(jnp.cumsum(tallies), jnp.arange(rows * top), side="right").astype(jnp.int32)
    table = members.reshape(top, rows).T
    table = table[jax.random.permutation(jax.random.fold_in(own, 1), rows)]
    turn = jax.random.randint(jax.random.fold_in(own, 2), (rows, 1), 0, top)
    return jnp.take_along_axis(table, (jnp.arange(top)[None, :] + turn) % top, axis=1)


def shares(amount, total, bound, skew, full):
    portions = [(1 << 20) // math.isqrt(grade ** skew) + 1 for grade in range(1, amount + 1)]
    largest = bound if full else min(bound, max(-(-total // amount), total * portions[0] // sum(portions)))
    least = 1 if total - largest >= amount - 1 else 0
    given, rest = [largest] + [least] * (amount - 1), total - largest - least * (amount - 1)
    while rest > 0:
        candidates = [i for i in range(1, amount) if given[i] < largest] or [i for i in range(1, amount) if given[i] < bound]
        whole, left = sum([portions[i] for i in candidates]), rest
        for i in candidates:
            addition = min(bound - given[i], max(1, left * portions[i] // whole), rest)
            given[i] = given[i] + addition
            rest = rest - addition
    return np.array(given)


def scatter_about(rng, shape, scale, most, shards=(), kind=jnp.bfloat16):
    level = levels(rng, shape, shards, -0.22, 0.18) if shards else 1.0
    values = jax.random.normal(rng, shape, jnp.float32) * scale * level
    return jnp.minimum(jnp.maximum(values, -most), most).astype(kind)


def gaussian_with(stream_key, shape, spread, reach, cuts, heavy, held_as=jnp.bfloat16):
    entries = spread * jax.random.normal(stream_key, shape, jnp.float32)
    if cuts:
        entries = entries * levels(stream_key, shape, cuts, -0.22, 0.18)
    return jnp.clip(strengthened(entries, jax.random.fold_in(stream_key, 3), *heavy), -reach, reach).astype(held_as)


def setup_inputs(seed: int = 0) -> dict:
    streams_of = jax.random.split(jax.random.key(seed), 10)
    query_in = scatter_about(streams_of[0], (TOKENS, CHAN), 1.0, 6.0, ((0, 16), (1, 2)))
    key_in = scatter_about(streams_of[1], (TOKENS, CHAN), 1.0, 6.0, ((0, 16), (1, 2)))
    value_in = scatter_about(streams_of[2], (TOKENS, CHAN), 1.0, 6.0, ((0, 16), (1, 2)))
    feat_filter = scatter_about(streams_of[3], (3, TAPS, CHAN), 0.4, 2.5, ((2, 2),), jnp.float32)
    inner_filter = scatter_about(streams_of[4], (TAPS, CHAN), 0.4, 2.5, ((1, 2),), jnp.float32)
    out_weight = gaussian_with(streams_of[5], (CHAN, OUTW), CHAN ** -0.5, 0.125, ((0, 2),), (0, 1, 2, 2.0))
    doc_pos = draw_doc_pos(jax.random.fold_in(streams_of[9], 71), 0)
    counts = uneven_parts(streams_of[7], N_DP, N_DP * NBLK - N_DP // 2, NBLK, 2).astype(jnp.int32)
    destination_keys = jax.random.split(jax.random.fold_in(streams_of[8], 1), (N_DP * NBLK) // NBLK)
    destination_turns = jax.random.permutation(jax.random.fold_in(streams_of[8], 3), (N_DP * NBLK) // NBLK)
    destination = jax.vmap(lambda own, number: shared_out(jax.random.fold_in(streams_of[8], 2), own, number, NBLK, N_DP, 1, 1, 2))(destination_keys, destination_turns).reshape((N_DP * NBLK, 1))
    return dict(query_in=query_in, key_in=key_in, value_in=value_in, feat_filter=feat_filter, inner_filter=inner_filter, out_weight=out_weight, doc_pos=doc_pos, counts=counts, destination=destination)


def featurize(extended, weights, positions):
    length = positions.shape[0]
    total = jnp.zeros((length, extended.shape[1]), jnp.float32)
    for offset in range(TAPS):
        shifted = extended[TAPS - 1 - offset:TAPS - 1 - offset + length].astype(jnp.float32)
        total = total + jnp.where((positions >= offset)[:, None], weights[offset][None, :] * shifted, 0.0)
    return total


def padded(columns):
    return jnp.concatenate([jnp.zeros((TAPS - 1, columns.shape[1]), columns.dtype), columns], axis=0)


def reference(query_in, key_in, value_in, feat_filter, inner_filter, out_weight, doc_pos, counts, destination):
    group_width = CHAN // N_TENSOR
    summed = jnp.zeros((TOKENS, OUTW), jnp.float32)
    for channel_group in range(N_TENSOR):
        lower = channel_group * group_width
        upper = lower + group_width
        feat_query = featurize(padded(query_in[:, lower:upper]), feat_filter[0, :, lower:upper], doc_pos)
        feat_key = featurize(padded(key_in[:, lower:upper]), feat_filter[1, :, lower:upper], doc_pos)
        feat_value = featurize(padded(value_in[:, lower:upper]), feat_filter[2, :, lower:upper], doc_pos)
        gated = feat_key * feat_value
        inner = featurize(padded(gated), inner_filter[:, lower:upper], doc_pos)
        mixed = (feat_query * inner).astype(jnp.bfloat16)
        part_sum = jnp.dot(mixed, out_weight[lower:upper], preferred_element_type=jnp.float32).astype(jnp.bfloat16)
        part_sum = lax.optimization_barrier(part_sum)
        summed = summed + part_sum.astype(jnp.float32)
    projected = summed.astype(jnp.bfloat16)
    blocks = projected.reshape(N_DP * NBLK, BLK, OUTW)
    source = jnp.arange(N_DP, dtype=jnp.int32)[:, None]
    block_index = jnp.arange(NBLK, dtype=jnp.int32)[None, :]
    target_dev = destination.reshape(N_DP, NBLK).astype(jnp.int32)
    filled = block_index < counts.astype(jnp.int32)[:, None]
    target = jnp.where(filled, target_dev * N_DP + source, N_DP * N_DP).astype(jnp.int32)
    result = jnp.zeros((N_DP * N_DP, BLK, OUTW), jnp.bfloat16)
    result = result.at[target.reshape(N_DP * NBLK)].set(blocks, mode="drop")
    return result.reshape(N_DP * N_DP * BLK, OUTW)
```

```python
import functools

import jax
import jax.numpy as jnp
from jax import lax
from jax.experimental import pallas as pl
from jax.experimental.pallas import tpu as pltpu
from jax.sharding import PartitionSpec as P

TAPS = 7
LEAD = 16
TILE = 32
LANES = 128


def taps_sum(ref, start, rows, weights, positions):
    total = None
    for offset in range(TAPS):
        term = weights[offset] * ref[start - offset : start - offset + rows, :]
        if positions is not None:
            term = jnp.where(positions >= offset, term, 0.0)
        total = term if total is None else total + term
    return total


def mix_kernel(
    slots, parts, width,
    block_of, clean, lead_clean, core,
    q_ref, k_ref, v_ref, qp_ref, kp_ref, vp_ref, tails_ref, pos_ref, feat_ref, inner_ref, w_hbm,
    *rest,
):
    outs, (qx, kx, vx, gx, mixed, w_ref, sem) = rest[:-7], rest[-7:]
    slot = pl.program_id(0)
    block_rows, channels = q_ref.shape
    tiles = block_rows // TILE
    w_copy = pltpu.make_async_copy(w_hbm, w_ref, sem)

    @pl.when(slot == 0)
    def _():
        w_copy.start()

    block = block_of[slot]
    base = pl.multiple_of(slot * block_rows, block_rows)

    @pl.when(block < 0)
    def _():
        mixed[pl.ds(base, block_rows), :] = jnp.zeros((block_rows, channels), mixed.dtype)

    @pl.when(block >= 0)
    def _():
        def one_chunk(c, carry):
            lanes = pl.ds(pl.multiple_of(c * LANES, LANES), LANES)
            for i, (dst, src, before) in enumerate(
                ((qx, q_ref, qp_ref), (kx, k_ref, kp_ref), (vx, v_ref, vp_ref))
            ):
                dst[LEAD:, :] = src[:, lanes].astype(jnp.float32)

                @pl.when(block == 0)
                def _():
                    dst[:LEAD, :] = tails_ref[i, :, lanes].astype(jnp.float32)

                @pl.when(block > 0)
                def _():
                    dst[:LEAD, :] = before[:, lanes].astype(jnp.float32)

            feat = [[feat_ref[i, t : t + 1, lanes] for t in range(TAPS)] for i in range(3)]
            inner = [inner_ref[t : t + 1, lanes] for t in range(TAPS)]

            def lead(masked):
                rows = 8
                positions = None
                if masked:
                    positions = pos_ref[0:1, :] - (
                        rows - lax.broadcasted_iota(jnp.int32, (rows, LANES), 0)
                    )
                gx[0:rows, :] = taps_sum(kx, LEAD - rows, rows, feat[1], positions) * taps_sum(
                    vx, LEAD - rows, rows, feat[2], positions
                )

            @pl.when(lead_clean[block] > 0)
            def _():
                lead(False)

            @pl.when(lead_clean[block] == 0)
            def _():
                lead(True)

            def tile_of(t, masked):
                first = t * TILE
                positions = pos_ref[first : first + TILE, :] if masked else None
                gx[8 + first : 8 + first + TILE, :] = taps_sum(
                    kx, LEAD + first, TILE, feat[1], positions
                ) * taps_sum(vx, LEAD + first, TILE, feat[2], positions)
                query = taps_sum(qx, LEAD + first, TILE, feat[0], positions)
                result = query * taps_sum(gx, 8 + first, TILE, inner, positions)
                mixed[pl.ds(pl.multiple_of(base + first, TILE), TILE), lanes] = result.astype(
                    mixed.dtype
                )

            for t in range(tiles):
                flag = clean[block * tiles + t]

                @pl.when(flag > 0)
                def _():
                    tile_of(t, False)

                @pl.when(flag == 0)
                def _():
                    tile_of(t, True)

            return carry

        lax.fori_loop(0, channels // LANES, one_chunk, 0)

    @pl.when(slot == slots - 1)
    def _():
        w_copy.wait()
        step = min(width, 512)
        for j in range(parts):
            first = lax.rem(core[0] + j, parts) * width if len(outs) > 1 else j * width

            def columns(n, carry):
                at = pl.multiple_of(first + n * step, step)
                part = jnp.dot(
                    mixed[...], w_ref[:, pl.ds(at, step)], preferred_element_type=jnp.float32
                ).astype(jnp.bfloat16)
                to = pl.ds(pl.multiple_of(n * step, step), step)
                if len(outs) > 1:
                    for s in range(slots):
                        outs[j][s, :, to] = part[s * block_rows : (s + 1) * block_rows]
                else:
                    outs[0][j, :, to] = part
                return carry

            lax.fori_loop(0, width // step, columns, 0)


def mix_blocks(scalars, streams, tails, positions, feat_filter, inner_filter, out_weight, parts, block_rows):
    slots = scalars[0].shape[0]
    rows, channels = streams[0].shape
    width = out_weight.shape[1] // parts
    lead_per_block = block_rows // LEAD

    def here(s, block_of, *_):
        return (jnp.maximum(block_of[s], 0), 0)

    def before(s, block_of, *_):
        return (jnp.maximum(block_of[s] * lead_per_block - 1, 0), 0)

    whole = lambda shape: pl.BlockSpec(shape, lambda *_: (0,) * len(shape))
    pair = parts == 2
    if pair:
        shapes = [jax.ShapeDtypeStruct((slots, block_rows, width), jnp.bfloat16)] * 2
    else:
        shapes = [jax.ShapeDtypeStruct((parts, slots * block_rows, width), jnp.bfloat16)]
    filled_flops = 2 * slots * block_rows * channels * out_weight.shape[1]
    return pl.pallas_call(
        functools.partial(mix_kernel, slots, parts, width),
        out_shape=shapes,
        grid_spec=pltpu.PrefetchScalarGridSpec(
            num_scalar_prefetch=4,
            grid=(slots,),
            in_specs=[pl.BlockSpec((block_rows, channels), here)] * 3
            + [pl.BlockSpec((LEAD, channels), before)] * 3
            + [
                whole(tails.shape),
                pl.BlockSpec((block_rows, LANES), here),
                whole(feat_filter.shape),
                whole(inner_filter.shape),
                pl.BlockSpec(memory_space=pl.ANY),
            ],
            out_specs=[whole(s.shape) for s in shapes],
            scratch_shapes=[pltpu.VMEM((LEAD + block_rows, LANES), jnp.float32)] * 3
            + [
                pltpu.VMEM((8 + block_rows, LANES), jnp.float32),
                pltpu.VMEM((slots * block_rows, channels), jnp.bfloat16),
                pltpu.VMEM(out_weight.shape, out_weight.dtype),
                pltpu.SemaphoreType.DMA,
            ],
        ),
        compiler_params=pltpu.CompilerParams(
            vmem_limit_bytes=48 * 1024 * 1024, dimension_semantics=("arbitrary",)
        ),
        cost_estimate=pl.CostEstimate(
            flops=filled_flops, bytes_accessed=16 * 1024 * 1024 + slots * 6 * 1024 * 1024, transcendentals=0
        ),
    )(*scalars, *streams, *streams, tails, positions, feat_filter, inner_filter, out_weight)


def per_device(
    query_in, key_in, value_in, feat_filter, inner_filter, out_weight, doc_pos, counts, destination
):
    row_count, channels = query_in.shape
    dp_count = lax.axis_size("dp")
    tp_count = lax.axis_size("tensor")
    me = lax.axis_index("dp")
    core = lax.axis_index("tensor").astype(jnp.int32).reshape(1)
    block_count = destination.shape[0]
    block_rows = row_count // block_count
    width = out_weight.shape[1] // tp_count
    streams = (query_in, key_in, value_in)

    tails = lax.ppermute(
        jnp.stack([x[row_count - LEAD :] for x in streams]),
        "dp",
        [(i, i + 1) for i in range(dp_count - 1)],
    )
    positions = jnp.broadcast_to(doc_pos[:, None], (row_count, LANES))
    clean = (jnp.min(doc_pos.reshape(-1, TILE), axis=1) >= TAPS - 1).astype(jnp.int32)
    lead_clean = (doc_pos.reshape(block_count, block_rows)[:, 0] >= 2 * (TAPS - 1)).astype(jnp.int32)

    half = dp_count // 2
    order = [r for pair in zip(range(half, dp_count), list(range(1, half)) + [0]) for r in pair]
    partner = jnp.bitwise_xor(me.astype(jnp.int32), jnp.asarray(order, jnp.int32))
    numbers = jnp.arange(block_count, dtype=jnp.int32)
    named = (destination[:, 0][None, :] == partner[:, None]) & (numbers < counts[0])[None, :]
    block_of = jnp.max(jnp.where(named, numbers[None, :], -1), axis=1)

    result = jnp.zeros((dp_count, block_rows, width), jnp.bfloat16)
    group = 2
    for first in range(0, dp_count, group):
        terms = mix_blocks(
            (block_of[first : first + group], clean, lead_clean, core),
            streams, tails, positions, feat_filter, inner_filter, out_weight, tp_count, block_rows,
        )
        if tp_count == 2:
            other = lax.ppermute(terms[1], "tensor", [(0, 1), (1, 0)])
        else:
            summed = lax.psum_scatter(terms[0], "tensor", scatter_dimension=0, tiled=False)
            summed = summed.reshape(group, block_rows, width)
        for s in range(group):
            r = order[first + s]
            if tp_count == 2:
                block = (
                    terms[0][s].astype(jnp.float32) + other[s].astype(jnp.float32)
                ).astype(jnp.bfloat16)
            else:
                block = summed[s]
            if r:
                block = lax.ppermute(block, "dp", [(i, i ^ r) for i in range(dp_count)])
            result = lax.dynamic_update_index_in_dim(result, block, jnp.bitwise_xor(me, r), 0)
    return result.reshape(dp_count * block_rows, width)


def solution(mesh):
    in_specs = (
        P("dp", "tensor"),
        P("dp", "tensor"),
        P("dp", "tensor"),
        P(None, None, "tensor"),
        P(None, "tensor"),
        P("tensor", None),
        P("dp"),
        P("dp"),
        P("dp", None),
    )
    return jax.shard_map(
        per_device, mesh=mesh, in_specs=in_specs, out_specs=P("dp", "tensor"), check_vma=False
    )
```

```python
import functools

import jax
import jax.numpy as jnp
from jax import lax
from jax.experimental import pallas as pl
from jax.experimental.pallas import tpu as pltpu
from jax.sharding import PartitionSpec as P

TAPS = 7
LEAD = 16
TILE = 32
LANES = 128


def taps_sum(ref, start, rows, weights, positions):
    total = None
    for offset in range(TAPS):
        term = weights[offset] * ref[start - offset : start - offset + rows, :]
        if positions is not None:
            term = jnp.where(positions >= offset, term, 0.0)
        total = term if total is None else total + term
    return total


def mix_kernel(
    slots, parts, width, before_rows, after_count,
    block_of, clean, core,
    q_ref, k_ref, v_ref, qp_ref, kp_ref, vp_ref, tails_ref, pos_ref, feat_ref, inner_ref,
    *rest,
):
    projects = before_rows > 0
    if projects:
        prior, w_hbm = rest[:2]
        mixed = rest[2 + after_count]
        outs = rest[3 + after_count : -6]
        qx, kx, vx, gx, w_ref, w_sem = rest[-6:]
    else:
        mixed = rest[after_count]
        qx, kx, vx, gx = rest[-4:]
    slot = pl.program_id(0)
    block_rows, channels = q_ref.shape
    steps = loop_steps(width, slots)
    columns = width // (slots * steps)
    chunks = channels // LANES // steps
    block = block_of[slot]

    def w_copy(j, at):
        start = lax.rem(core[0] + j, parts) * width if parts == 2 else j * width
        span = pl.ds(pl.multiple_of(start + at * columns, LANES), columns)
        return pltpu.make_async_copy(w_hbm.at[:, span], w_ref.at[:, span], w_sem.at[at, j]), span

    if projects:

        @pl.when(slot == 0)
        def _():
            for at in range(slots * steps):
                for j in range(parts):
                    w_copy(j, at)[0].start()

    def project(i):
        if not projects:
            return
        at = slot * steps + i
        to = pl.ds(pl.multiple_of(at * columns, LANES), columns)
        for j in range(parts):
            copy, span = w_copy(j, at)
            copy.wait()
            part = jnp.dot(
                prior[...], w_ref[:, span], preferred_element_type=jnp.float32
            ).astype(jnp.bfloat16)
            if parts == 2:
                for s in range(before_rows // block_rows):
                    outs[j][s, :, to] = part[s * block_rows : (s + 1) * block_rows]
            else:
                outs[0][j, :, to] = part

    def convolve(masked, c):
        lanes = pl.ds(pl.multiple_of(c * LANES, LANES), LANES)
        for i, (dst, src, before) in enumerate(
            ((qx, q_ref, qp_ref), (kx, k_ref, kp_ref), (vx, v_ref, vp_ref))
        ):
            tail = tails_ref[i, :, lanes].astype(jnp.float32)
            dst[:LEAD, :] = jnp.where(block == 0, tail, before[:, lanes].astype(jnp.float32))
            dst[LEAD:, :] = src[:, lanes].astype(jnp.float32)
        feat = [[feat_ref[i, t : t + 1, lanes] for t in range(TAPS)] for i in range(3)]
        inner = [inner_ref[t : t + 1, lanes] for t in range(TAPS)]
        rows = 8
        positions = None
        if masked:
            positions = pos_ref[0:1, :] - (
                rows - lax.broadcasted_iota(jnp.int32, (rows, LANES), 0)
            )
        gx[0:rows, :] = taps_sum(kx, LEAD - rows, rows, feat[1], positions) * taps_sum(
            vx, LEAD - rows, rows, feat[2], positions
        )
        for first in range(0, block_rows, TILE):
            positions = pos_ref[first : first + TILE, :] if masked else None
            gx[8 + first : 8 + first + TILE, :] = taps_sum(
                kx, LEAD + first, TILE, feat[1], positions
            ) * taps_sum(vx, LEAD + first, TILE, feat[2], positions)
            query = taps_sum(qx, LEAD + first, TILE, feat[0], positions)
            result = query * taps_sum(gx, 8 + first, TILE, inner, positions)
            mixed[first : first + TILE, lanes] = result.astype(mixed.dtype)

    def body(masked, i, carry):
        project(i)
        if masked is not None:
            for c in range(chunks):
                convolve(masked, i * chunks + c)
        return carry

    @pl.when(block < 0)
    def _():
        mixed[...] = jnp.zeros_like(mixed)
        lax.fori_loop(0, steps, functools.partial(body, None), 0)

    unmasked = clean[jnp.maximum(block, 0)] > 0

    @pl.when((block >= 0) & unmasked)
    def _():
        lax.fori_loop(0, steps, functools.partial(body, False), 0)

    @pl.when((block >= 0) & jnp.logical_not(unmasked))
    def _():
        lax.fori_loop(0, steps, functools.partial(body, True), 0)


def loop_steps(width, slots):
    return next(n for n in (4, 2, 1) if width % (n * slots * LANES) == 0)


def mix_blocks(
    block_of, clean, core, streams, tails, positions, feat_filter, inner_filter, prior, out_weight,
    parts, block_rows, after,
):
    slots = block_of.shape[0]
    channels = streams[0].shape[1]
    width = out_weight.shape[1] // parts
    lead_per_block = block_rows // LEAD
    before_rows = 0 if prior is None else prior.shape[0]

    def here(s, block_of, *_):
        return (jnp.maximum(block_of[s], 0), 0)

    def before(s, block_of, *_):
        return (jnp.maximum(block_of[s] * lead_per_block - 1, 0), 0)

    whole = lambda shape: pl.BlockSpec(shape, lambda *_: (0,) * len(shape))
    shapes, operands, specs, scratch = [], [], [], []
    if prior is not None:
        operands = [prior, out_weight]
        specs = [whole(prior.shape), pl.BlockSpec(memory_space=pl.ANY)]
        scratch = [
            pltpu.VMEM(out_weight.shape, out_weight.dtype),
            pltpu.SemaphoreType.DMA((slots * loop_steps(width, slots), parts)),
        ]
        if parts == 2:
            shapes = [(before_rows // block_rows, block_rows, width)] * 2
        else:
            shapes = [(parts, before_rows, width)]
    return pl.pallas_call(
        functools.partial(mix_kernel, slots, parts, width, before_rows, len(after)),
        out_shape=[
            jax.ShapeDtypeStruct(shape, jnp.bfloat16)
            for shape in [(slots * block_rows, channels)] + shapes
        ],
        grid_spec=pltpu.PrefetchScalarGridSpec(
            num_scalar_prefetch=3,
            grid=(slots,),
            in_specs=[pl.BlockSpec((block_rows, channels), here)] * 3
            + [pl.BlockSpec((LEAD, channels), before)] * 3
            + [
                whole(tails.shape),
                pl.BlockSpec((block_rows, LANES), here),
                whole(feat_filter.shape),
                whole(inner_filter.shape),
            ]
            + specs
            + [pl.BlockSpec(memory_space=pl.ANY)] * len(after),
            out_specs=[pl.BlockSpec((block_rows, channels), lambda s, *_: (s, 0))]
            + [whole(shape) for shape in shapes],
            scratch_shapes=[pltpu.VMEM((LEAD + block_rows, LANES), jnp.float32)] * 3
            + [pltpu.VMEM((8 + block_rows, LANES), jnp.float32)]
            + scratch,
        ),
        compiler_params=pltpu.CompilerParams(
            vmem_limit_bytes=48 * 1024 * 1024, dimension_semantics=("arbitrary",)
        ),
        cost_estimate=pl.CostEstimate(
            flops=2 * before_rows * channels * out_weight.shape[1],
            bytes_accessed=16 * 1024 * 1024 + slots * 6 * 1024 * 1024,
            transcendentals=0,
        ),
    )(
        block_of, clean, core, *streams, *streams, tails, positions, feat_filter, inner_filter,
        *operands, *after,
    )


def per_device(
    query_in, key_in, value_in, feat_filter, inner_filter, out_weight, doc_pos, counts, destination
):
    row_count, channels = query_in.shape
    dp_count = lax.axis_size("dp")
    tp_count = lax.axis_size("tensor")
    me = lax.axis_index("dp")
    core = lax.axis_index("tensor").astype(jnp.int32).reshape(1)
    block_count = destination.shape[0]
    block_rows = row_count // block_count
    width = out_weight.shape[1] // tp_count
    streams = (query_in, key_in, value_in)

    tails = lax.ppermute(
        jnp.stack([x[row_count - LEAD :] for x in streams]),
        "dp",
        [(i, i + 1) for i in range(dp_count - 1)],
    )
    positions = jnp.broadcast_to(doc_pos[:, None], (row_count, LANES))
    by_block = doc_pos.reshape(block_count, block_rows)
    clean = (jnp.min(by_block, axis=1) >= TAPS - 1) & (by_block[:, 0] >= 2 * (TAPS - 1))
    clean = clean.astype(jnp.int32)

    half = dp_count // 2
    far, near = list(range(half, dp_count)), list(range(1, half)) + [0]
    order = far[:1] + [r for pair in zip(far[1:], near) for r in pair] + near[half - 1 :]
    sizes = [1] + [2] * (half - 1) + [1]
    partner = jnp.bitwise_xor(me.astype(jnp.int32), jnp.asarray(order, jnp.int32))
    numbers = jnp.arange(block_count, dtype=jnp.int32)
    named = (destination[:, 0][None, :] == partner[:, None]) & (numbers < counts[0])[None, :]
    block_of = jnp.max(jnp.where(named, numbers[None, :], -1), axis=1)

    ready = []
    arrived = []
    result = jnp.zeros((dp_count, block_rows, width), jnp.bfloat16)
    firsts = [sum(sizes[:g]) for g in range(len(sizes))]
    slots_of = [block_of[f : f + n] for f, n in zip(firsts, sizes)]
    slots_of.append(jnp.full((1,), -1, jnp.int32))

    def blocks_after(g, prior, after):
        return mix_blocks(
            slots_of[g], clean, core, streams, tails, positions, feat_filter, inner_filter, prior,
            out_weight, tp_count, block_rows, after,
        )

    (mixed,) = blocks_after(0, None, [])
    for g, group in enumerate(sizes):
        first = firsts[g]
        mixed, *terms = blocks_after(g + 1, mixed, ready[-2] if len(ready) > 1 else [])
        ready.append([])
        arrived.append([])
        if tp_count == 2:
            other = lax.ppermute(terms[1], "tensor", [(0, 1), (1, 0)])
        else:
            summed = lax.psum_scatter(terms[0], "tensor", scatter_dimension=0, tiled=False)
            summed = summed.reshape(group, block_rows, width)
        for s in range(group):
            r = order[first + s]
            if tp_count == 2:
                block = (
                    terms[0][s].astype(jnp.float32) + other[s].astype(jnp.float32)
                ).astype(jnp.bfloat16)
            else:
                block = summed[s]
            ready[-1].append(block)
            if r:
                block = lax.ppermute(block, "dp", [(i, i ^ r) for i in range(dp_count)])
                arrived[-1].append(block)
            result = lax.dynamic_update_index_in_dim(result, block, jnp.bitwise_xor(me, r), 0)
    return result.reshape(dp_count * block_rows, width)


def solution(mesh):
    in_specs = (
        P("dp", "tensor"),
        P("dp", "tensor"),
        P("dp", "tensor"),
        P(None, None, "tensor"),
        P(None, "tensor"),
        P("tensor", None),
        P("dp"),
        P("dp"),
        P("dp", None),
    )
    return jax.shard_map(
        per_device, mesh=mesh, in_specs=in_specs, out_specs=P("dp", "tensor"), check_vma=False
    )
```

```python
import functools

import jax
import jax.numpy as jnp
from jax import lax
from jax.experimental import pallas as pl
from jax.experimental.pallas import tpu as pltpu
from jax.sharding import PartitionSpec as P

TAPS = 7
LEAD = 16
TILE = 32
LANES = 128


def taps_sum(ref, start, rows, weights, positions):
    total = None
    for offset in range(TAPS):
        term = weights[offset] * ref[start - offset : start - offset + rows, :]
        if positions is not None:
            term = jnp.where(positions >= offset, term, 0.0)
        total = term if total is None else total + term
    return total


def mix_kernel(
    slots, parts, width, after_count,
    block_of, clean, lead_clean, core,
    q_ref, k_ref, v_ref, qp_ref, kp_ref, vp_ref, tails_ref, pos_ref, feat_ref, inner_ref, w_hbm,
    *rest,
):
    scratch, outs = rest[-7:], rest[after_count:-7]
    qx, kx, vx, gx, mixed, w_ref, sem = scratch
    slot = pl.program_id(0)
    block_rows, channels = q_ref.shape
    tiles = block_rows // TILE
    w_copy = pltpu.make_async_copy(w_hbm, w_ref, sem)

    @pl.when(slot == 0)
    def _():
        w_copy.start()

    block = block_of[slot]
    base = pl.multiple_of(slot * block_rows, block_rows)

    @pl.when(block < 0)
    def _():
        mixed[pl.ds(base, block_rows), :] = jnp.zeros((block_rows, channels), mixed.dtype)

    @pl.when(block >= 0)
    def _():
        at_start = block == 0

        def one_chunk(masked, c, carry):
            lanes = pl.ds(pl.multiple_of(c * LANES, LANES), LANES)
            for i, (dst, src, before) in enumerate(
                ((qx, q_ref, qp_ref), (kx, k_ref, kp_ref), (vx, v_ref, vp_ref))
            ):
                tail = tails_ref[i, :, lanes].astype(jnp.float32)
                dst[:LEAD, :] = jnp.where(at_start, tail, before[:, lanes].astype(jnp.float32))
                dst[LEAD:, :] = src[:, lanes].astype(jnp.float32)

            feat = [[feat_ref[i, t : t + 1, lanes] for t in range(TAPS)] for i in range(3)]
            inner = [inner_ref[t : t + 1, lanes] for t in range(TAPS)]
            rows = 8
            positions = None
            if masked:
                positions = pos_ref[0:1, :] - (
                    rows - lax.broadcasted_iota(jnp.int32, (rows, LANES), 0)
                )
            gx[0:rows, :] = taps_sum(kx, LEAD - rows, rows, feat[1], positions) * taps_sum(
                vx, LEAD - rows, rows, feat[2], positions
            )

            def tile_of(first, rows, masked):
                positions = pos_ref[first : first + rows, :] if masked else None
                gx[8 + first : 8 + first + rows, :] = taps_sum(
                    kx, LEAD + first, rows, feat[1], positions
                ) * taps_sum(vx, LEAD + first, rows, feat[2], positions)
                query = taps_sum(qx, LEAD + first, rows, feat[0], positions)
                result = query * taps_sum(gx, 8 + first, rows, inner, positions)
                mixed[pl.ds(pl.multiple_of(base + first, TILE), rows), lanes] = result.astype(
                    mixed.dtype
                )

            if not masked:
                for t in range(tiles):
                    tile_of(t * TILE, TILE, False)
                return carry
            for t in range(tiles):
                flag = clean[block * tiles + t]

                @pl.when(flag > 0)
                def _():
                    tile_of(t * TILE, TILE, False)

                @pl.when(flag == 0)
                def _():
                    tile_of(t * TILE, TILE, True)

            return carry

        whole_clean = lead_clean[block]
        for t in range(tiles):
            whole_clean = whole_clean * clean[block * tiles + t]

        @pl.when(whole_clean > 0)
        def _():
            lax.fori_loop(0, channels // LANES, functools.partial(one_chunk, False), 0)

        @pl.when(whole_clean == 0)
        def _():
            lax.fori_loop(0, channels // LANES, functools.partial(one_chunk, True), 0)

    @pl.when(slot == slots - 1)
    def _():
        w_copy.wait()
        step = min(width, 1024)
        for j in range(parts):
            first = lax.rem(core[0] + j, parts) * width if len(outs) > 1 else j * width

            def columns(n, carry):
                at = pl.multiple_of(first + n * step, step)
                part = jnp.dot(
                    mixed[...], w_ref[:, pl.ds(at, step)], preferred_element_type=jnp.float32
                ).astype(jnp.bfloat16)
                to = pl.ds(pl.multiple_of(n * step, step), step)
                if len(outs) > 1:
                    for s in range(slots):
                        outs[j][s, :, to] = part[s * block_rows : (s + 1) * block_rows]
                else:
                    outs[0][j, :, to] = part
                return carry

            lax.fori_loop(0, width // step, columns, 0)


def mix_blocks(scalars, streams, tails, positions, feat_filter, inner_filter, out_weight, parts, block_rows, after):
    slots = scalars[0].shape[0]
    rows, channels = streams[0].shape
    width = out_weight.shape[1] // parts
    lead_per_block = block_rows // LEAD

    def here(s, block_of, *_):
        return (jnp.maximum(block_of[s], 0), 0)

    def before(s, block_of, *_):
        return (jnp.maximum(block_of[s] * lead_per_block - 1, 0), 0)

    whole = lambda shape: pl.BlockSpec(shape, lambda *_: (0,) * len(shape))
    pair = parts == 2
    if pair:
        shapes = [jax.ShapeDtypeStruct((slots, block_rows, width), jnp.bfloat16)] * 2
    else:
        shapes = [jax.ShapeDtypeStruct((parts, slots * block_rows, width), jnp.bfloat16)]
    filled_flops = 2 * slots * block_rows * channels * out_weight.shape[1]
    return pl.pallas_call(
        functools.partial(mix_kernel, slots, parts, width, len(after)),
        out_shape=shapes,
        grid_spec=pltpu.PrefetchScalarGridSpec(
            num_scalar_prefetch=4,
            grid=(slots,),
            in_specs=[pl.BlockSpec((block_rows, channels), here)] * 3
            + [pl.BlockSpec((LEAD, channels), before)] * 3
            + [
                whole(tails.shape),
                pl.BlockSpec((block_rows, LANES), here),
                whole(feat_filter.shape),
                whole(inner_filter.shape),
            ]
            + [pl.BlockSpec(memory_space=pl.ANY)] * (1 + len(after)),
            out_specs=[whole(s.shape) for s in shapes],
            scratch_shapes=[pltpu.VMEM((LEAD + block_rows, LANES), jnp.float32)] * 3
            + [
                pltpu.VMEM((8 + block_rows, LANES), jnp.float32),
                pltpu.VMEM((slots * block_rows, channels), jnp.bfloat16),
                pltpu.VMEM(out_weight.shape, out_weight.dtype),
                pltpu.SemaphoreType.DMA,
            ],
        ),
        compiler_params=pltpu.CompilerParams(
            vmem_limit_bytes=48 * 1024 * 1024, dimension_semantics=("arbitrary",)
        ),
        cost_estimate=pl.CostEstimate(
            flops=filled_flops, bytes_accessed=16 * 1024 * 1024 + slots * 6 * 1024 * 1024, transcendentals=0
        ),
    )(*scalars, *streams, *streams, tails, positions, feat_filter, inner_filter, out_weight, *after)


def unset_kernel(out):
    pass


def unset(shape, dtype):
    return pl.pallas_call(
        unset_kernel,
        out_shape=jax.ShapeDtypeStruct(shape, dtype),
        out_specs=pl.BlockSpec(memory_space=pl.ANY),
        cost_estimate=pl.CostEstimate(flops=0, bytes_accessed=0, transcendentals=0),
    )()


def per_device(
    query_in, key_in, value_in, feat_filter, inner_filter, out_weight, doc_pos, counts, destination
):
    row_count, channels = query_in.shape
    dp_count = lax.axis_size("dp")
    tp_count = lax.axis_size("tensor")
    me = lax.axis_index("dp")
    core = lax.axis_index("tensor").astype(jnp.int32).reshape(1)
    block_count = destination.shape[0]
    block_rows = row_count // block_count
    width = out_weight.shape[1] // tp_count
    streams = (query_in, key_in, value_in)

    tails = lax.ppermute(
        jnp.stack([x[row_count - LEAD :] for x in streams]),
        "dp",
        [(i, i + 1) for i in range(dp_count - 1)],
    )
    positions = jnp.broadcast_to(doc_pos[:, None], (row_count, LANES))
    clean = (jnp.min(doc_pos.reshape(-1, TILE), axis=1) >= TAPS - 1).astype(jnp.int32)
    lead_clean = (doc_pos.reshape(block_count, block_rows)[:, 0] >= 2 * (TAPS - 1)).astype(jnp.int32)

    half = dp_count // 2
    far, near = list(range(half, dp_count)), list(range(1, half)) + [0]
    order = far[:1] + [r for pair in zip(far[1:], near) for r in pair] + near[half - 1 :]
    sizes = [1] + [2] * (half - 2) + [3]
    partner = jnp.bitwise_xor(me.astype(jnp.int32), jnp.asarray(order, jnp.int32))
    numbers = jnp.arange(block_count, dtype=jnp.int32)
    named = (destination[:, 0][None, :] == partner[:, None]) & (numbers < counts[0])[None, :]
    block_of = jnp.max(jnp.where(named, numbers[None, :], -1), axis=1)

    ready = []
    arrived = []
    result = unset((dp_count, block_rows, width), jnp.bfloat16)
    first = 0
    for group in sizes:
        terms = mix_blocks(
            (block_of[first : first + group], clean, lead_clean, core),
            streams, tails, positions, feat_filter, inner_filter, out_weight, tp_count, block_rows,
            ready[-2] if len(ready) > 1 else [],
        )
        ready.append([])
        arrived.append([])
        if tp_count == 2:
            other = lax.ppermute(terms[1], "tensor", [(0, 1), (1, 0)])
        else:
            summed = lax.psum_scatter(terms[0], "tensor", scatter_dimension=0, tiled=False)
            summed = summed.reshape(group, block_rows, width)
        for s in range(group):
            r = order[first + s]
            if tp_count == 2:
                block = (
                    terms[0][s].astype(jnp.float32) + other[s].astype(jnp.float32)
                ).astype(jnp.bfloat16)
            else:
                block = summed[s]
            ready[-1].append(block)
            if r:
                block = lax.ppermute(block, "dp", [(i, i ^ r) for i in range(dp_count)])
                arrived[-1].append(block)
            result = lax.dynamic_update_index_in_dim(result, block, jnp.bitwise_xor(me, r), 0)
        first += group
    return result.reshape(dp_count * block_rows, width)


def solution(mesh):
    in_specs = (
        P("dp", "tensor"),
        P("dp", "tensor"),
        P("dp", "tensor"),
        P(None, None, "tensor"),
        P(None, "tensor"),
        P("tensor", None),
        P("dp"),
        P("dp"),
        P("dp", None),
    )
    return jax.shard_map(
        per_device, mesh=mesh, in_specs=in_specs, out_specs=P("dp", "tensor"), check_vma=False
    )
```

```python
import functools

import jax
import jax.numpy as jnp
from jax import lax
from jax.experimental import pallas as pl
from jax.experimental.pallas import tpu as pltpu
from jax.sharding import PartitionSpec as P

TAPS = 7
LEAD = 16
TILE = 32
LANES = 128


def taps_sum(ref, start, rows, weights, positions):
    total = None
    for offset in range(TAPS):
        term = weights[offset] * ref[start - offset : start - offset + rows, :]
        if positions is not None:
            term = jnp.where(positions >= offset, term, 0.0)
        total = term if total is None else total + term
    return total


def mix_kernel(
    slots, parts, width, after_count,
    block_of, clean, lead_clean, core,
    q_ref, k_ref, v_ref, qp_ref, kp_ref, vp_ref, tails_ref, pos_ref, feat_ref, inner_ref, w_hbm,
    *rest,
):
    scratch, outs = rest[-7:], rest[after_count:-7]
    qx, kx, vx, gx, mixed, w_ref, sem = scratch
    slot = pl.program_id(0)
    block_rows, channels = q_ref.shape
    tiles = block_rows // TILE
    w_copy = pltpu.make_async_copy(w_hbm, w_ref, sem)

    @pl.when(slot == 0)
    def _():
        w_copy.start()

    block = block_of[slot]
    base = pl.multiple_of(slot * block_rows, block_rows)

    @pl.when(block < 0)
    def _():
        mixed[pl.ds(base, block_rows), :] = jnp.zeros((block_rows, channels), mixed.dtype)

    @pl.when(block >= 0)
    def _():
        at_start = block == 0

        def one_chunk(masked, c, carry):
            lanes = pl.ds(pl.multiple_of(c * LANES, LANES), LANES)
            for i, (dst, src, before) in enumerate(
                ((qx, q_ref, qp_ref), (kx, k_ref, kp_ref), (vx, v_ref, vp_ref))
            ):
                tail = tails_ref[i, :, lanes].astype(jnp.float32)
                dst[:LEAD, :] = jnp.where(at_start, tail, before[:, lanes].astype(jnp.float32))
                dst[LEAD:, :] = src[:, lanes].astype(jnp.float32)

            feat = [[feat_ref[i, t : t + 1, lanes] for t in range(TAPS)] for i in range(3)]
            inner = [inner_ref[t : t + 1, lanes] for t in range(TAPS)]
            rows = 8
            positions = None
            if masked:
                positions = pos_ref[0:1, :] - (
                    rows - lax.broadcasted_iota(jnp.int32, (rows, LANES), 0)
                )
            gx[0:rows, :] = taps_sum(kx, LEAD - rows, rows, feat[1], positions) * taps_sum(
                vx, LEAD - rows, rows, feat[2], positions
            )

            def tile_of(first, rows, masked):
                positions = pos_ref[first : first + rows, :] if masked else None
                gx[8 + first : 8 + first + rows, :] = taps_sum(
                    kx, LEAD + first, rows, feat[1], positions
                ) * taps_sum(vx, LEAD + first, rows, feat[2], positions)
                query = taps_sum(qx, LEAD + first, rows, feat[0], positions)
                result = query * taps_sum(gx, 8 + first, rows, inner, positions)
                mixed[pl.ds(pl.multiple_of(base + first, TILE), rows), lanes] = result.astype(
                    mixed.dtype
                )

            if not masked:
                for t in range(tiles):
                    tile_of(t * TILE, TILE, False)
                return carry
            for t in range(tiles):
                flag = clean[block * tiles + t]

                @pl.when(flag > 0)
                def _():
                    tile_of(t * TILE, TILE, False)

                @pl.when(flag == 0)
                def _():
                    tile_of(t * TILE, TILE, True)

            return carry

        whole_clean = lead_clean[block]
        for t in range(tiles):
            whole_clean = whole_clean * clean[block * tiles + t]

        @pl.when(whole_clean > 0)
        def _():
            lax.fori_loop(0, channels // LANES, functools.partial(one_chunk, False), 0)

        @pl.when(whole_clean == 0)
        def _():
            lax.fori_loop(0, channels // LANES, functools.partial(one_chunk, True), 0)

    @pl.when(slot == slots - 1)
    def _():
        w_copy.wait()
        step = min(width, 1024)
        for j in range(parts):
            first = lax.rem(core[0] + j, parts) * width if len(outs) > 1 else j * width

            def columns(n, carry):
                at = pl.multiple_of(first + n * step, step)
                part = jnp.dot(
                    mixed[...], w_ref[:, pl.ds(at, step)], preferred_element_type=jnp.float32
                ).astype(jnp.bfloat16)
                to = pl.ds(pl.multiple_of(n * step, step), step)
                if len(outs) > 1:
                    for s in range(slots):
                        outs[j][s, :, to] = part[s * block_rows : (s + 1) * block_rows]
                else:
                    outs[0][j, :, to] = part
                return carry

            lax.fori_loop(0, width // step, columns, 0)


def mix_blocks(scalars, streams, tails, positions, feat_filter, inner_filter, out_weight, parts, block_rows, after):
    slots = scalars[0].shape[0]
    rows, channels = streams[0].shape
    width = out_weight.shape[1] // parts
    lead_per_block = block_rows // LEAD

    def here(s, block_of, *_):
        return (jnp.maximum(block_of[s], 0), 0)

    def before(s, block_of, *_):
        return (jnp.maximum(block_of[s] * lead_per_block - 1, 0), 0)

    whole = lambda shape: pl.BlockSpec(shape, lambda *_: (0,) * len(shape))
    pair = parts == 2
    if pair:
        shapes = [jax.ShapeDtypeStruct((slots, block_rows, width), jnp.bfloat16)] * 2
    else:
        shapes = [jax.ShapeDtypeStruct((parts, slots * block_rows, width), jnp.bfloat16)]
    filled_flops = 2 * slots * block_rows * channels * out_weight.shape[1]
    return pl.pallas_call(
        functools.partial(mix_kernel, slots, parts, width, len(after)),
        out_shape=shapes,
        grid_spec=pltpu.PrefetchScalarGridSpec(
            num_scalar_prefetch=4,
            grid=(slots,),
            in_specs=[pl.BlockSpec((block_rows, channels), here)] * 3
            + [pl.BlockSpec((LEAD, channels), before)] * 3
            + [
                whole(tails.shape),
                pl.BlockSpec((block_rows, LANES), here),
                whole(feat_filter.shape),
                whole(inner_filter.shape),
            ]
            + [pl.BlockSpec(memory_space=pl.ANY)] * (1 + len(after)),
            out_specs=[whole(s.shape) for s in shapes],
            scratch_shapes=[pltpu.VMEM((LEAD + block_rows, LANES), jnp.float32)] * 3
            + [
                pltpu.VMEM((8 + block_rows, LANES), jnp.float32),
                pltpu.VMEM((slots * block_rows, channels), jnp.bfloat16),
                pltpu.VMEM(out_weight.shape, out_weight.dtype),
                pltpu.SemaphoreType.DMA,
            ],
        ),
        compiler_params=pltpu.CompilerParams(
            vmem_limit_bytes=48 * 1024 * 1024, dimension_semantics=("arbitrary",)
        ),
        cost_estimate=pl.CostEstimate(
            flops=filled_flops, bytes_accessed=16 * 1024 * 1024 + slots * 6 * 1024 * 1024, transcendentals=0
        ),
    )(*scalars, *streams, *streams, tails, positions, feat_filter, inner_filter, out_weight, *after)


def unset_kernel(out):
    pass


def unset(shape, dtype):
    return pl.pallas_call(
        unset_kernel,
        out_shape=jax.ShapeDtypeStruct(shape, dtype),
        out_specs=pl.BlockSpec(memory_space=pl.ANY),
        cost_estimate=pl.CostEstimate(flops=0, bytes_accessed=0, transcendentals=0),
    )()


def per_device(
    query_in, key_in, value_in, feat_filter, inner_filter, out_weight, doc_pos, counts, destination
):
    row_count, channels = query_in.shape
    dp_count = lax.axis_size("dp")
    tp_count = lax.axis_size("tensor")
    me = lax.axis_index("dp")
    core = lax.axis_index("tensor").astype(jnp.int32).reshape(1)
    block_count = destination.shape[0]
    block_rows = row_count // block_count
    width = out_weight.shape[1] // tp_count
    streams = (query_in, key_in, value_in)

    tails = lax.ppermute(
        jnp.stack([x[row_count - LEAD :] for x in streams]),
        "dp",
        [(i, i + 1) for i in range(dp_count - 1)],
    )
    positions = jnp.broadcast_to(doc_pos[:, None], (row_count, LANES))
    clean = (jnp.min(doc_pos.reshape(-1, TILE), axis=1) >= TAPS - 1).astype(jnp.int32)
    lead_clean = (doc_pos.reshape(block_count, block_rows)[:, 0] >= 2 * (TAPS - 1)).astype(jnp.int32)

    half = dp_count // 2
    far, near = list(range(half, dp_count)), list(range(1, half)) + [0]
    groups, at = [far[:1]], 0
    for k in range(1, half - 1):
        to = at + (2 if k == 3 else 1)
        groups.append([far[k]] + near[at:to])
        at = to
    groups.append(far[half - 1 :] + near[at:])
    order = [r for group in groups for r in group]
    sizes = [len(group) for group in groups]
    partner = jnp.bitwise_xor(me.astype(jnp.int32), jnp.asarray(order, jnp.int32))
    numbers = jnp.arange(block_count, dtype=jnp.int32)
    named = (destination[:, 0][None, :] == partner[:, None]) & (numbers < counts[0])[None, :]
    block_of = jnp.max(jnp.where(named, numbers[None, :], -1), axis=1)

    ready = []
    arrived = []
    result = unset((dp_count, block_rows, width), jnp.bfloat16)
    first = 0
    for group in sizes:
        terms = mix_blocks(
            (block_of[first : first + group], clean, lead_clean, core),
            streams, tails, positions, feat_filter, inner_filter, out_weight, tp_count, block_rows,
            ready[-2] if len(ready) > 1 else [],
        )
        ready.append([])
        arrived.append([])
        if tp_count == 2:
            other = lax.ppermute(terms[1], "tensor", [(0, 1), (1, 0)])
        else:
            summed = lax.psum_scatter(terms[0], "tensor", scatter_dimension=0, tiled=False)
            summed = summed.reshape(group, block_rows, width)
        for s in range(group):
            r = order[first + s]
            if tp_count == 2:
                block = (
                    terms[0][s].astype(jnp.float32) + other[s].astype(jnp.float32)
                ).astype(jnp.bfloat16)
            else:
                block = summed[s]
            ready[-1].append(block)
            if r:
                block = lax.ppermute(block, "dp", [(i, i ^ r) for i in range(dp_count)])
                arrived[-1].append(block)
            result = lax.dynamic_update_index_in_dim(result, block, jnp.bitwise_xor(me, r), 0)
        first += group
    return result.reshape(dp_count * block_rows, width)


def solution(mesh):
    in_specs = (
        P("dp", "tensor"),
        P("dp", "tensor"),
        P("dp", "tensor"),
        P(None, None, "tensor"),
        P(None, "tensor"),
        P("tensor", None),
        P("dp"),
        P("dp"),
        P("dp", None),
    )
    return jax.shard_map(
        per_device, mesh=mesh, in_specs=in_specs, out_specs=P("dp", "tensor"), check_vma=False
    )
```

```python
import functools

import jax
import jax.numpy as jnp
from jax import lax
from jax.experimental import pallas as pl
from jax.experimental.pallas import tpu as pltpu
from jax.sharding import PartitionSpec as P

TAPS = 7
LEAD = 16
TILE = 32
LANES = 128


def taps_sum(ref, start, rows, weights, positions):
    total = None
    for offset in range(TAPS):
        term = weights[offset] * ref[start - offset : start - offset + rows, :]
        if positions is not None:
            term = jnp.where(positions >= offset, term, 0.0)
        total = term if total is None else total + term
    return total


def mix_kernel(
    slots, parts, width, after_count,
    block_of, clean, lead_clean, core,
    q_ref, k_ref, v_ref, qp_ref, kp_ref, vp_ref, tails_ref, pos_ref, feat_ref, inner_ref, w_hbm,
    *rest,
):
    scratch, outs = rest[-7:], rest[after_count:-7]
    qx, kx, vx, gx, mixed, w_ref, sem = scratch
    slot = pl.program_id(0)
    block_rows, channels = q_ref.shape
    tiles = block_rows // TILE
    w_copy = pltpu.make_async_copy(w_hbm, w_ref, sem)

    @pl.when(slot == 0)
    def _():
        w_copy.start()

    block = block_of[slot]
    base = pl.multiple_of(slot * block_rows, block_rows)

    @pl.when(block < 0)
    def _():
        mixed[pl.ds(base, block_rows), :] = jnp.zeros((block_rows, channels), mixed.dtype)

    @pl.when(block >= 0)
    def _():
        at_start = block == 0

        def one_chunk(masked, c, carry):
            lanes = pl.ds(pl.multiple_of(c * LANES, LANES), LANES)
            for i, (dst, src, before) in enumerate(
                ((qx, q_ref, qp_ref), (kx, k_ref, kp_ref), (vx, v_ref, vp_ref))
            ):
                tail = tails_ref[i, :, lanes].astype(jnp.float32)
                dst[:LEAD, :] = jnp.where(at_start, tail, before[:, lanes].astype(jnp.float32))
                dst[LEAD:, :] = src[:, lanes].astype(jnp.float32)

            feat = [[feat_ref[i, t : t + 1, lanes] for t in range(TAPS)] for i in range(3)]
            inner = [inner_ref[t : t + 1, lanes] for t in range(TAPS)]
            rows = 8
            positions = None
            if masked:
                positions = pos_ref[0:1, :] - (
                    rows - lax.broadcasted_iota(jnp.int32, (rows, LANES), 0)
                )
            gx[0:rows, :] = taps_sum(kx, LEAD - rows, rows, feat[1], positions) * taps_sum(
                vx, LEAD - rows, rows, feat[2], positions
            )

            def tile_of(first, rows, masked):
                positions = pos_ref[first : first + rows, :] if masked else None
                gx[8 + first : 8 + first + rows, :] = taps_sum(
                    kx, LEAD + first, rows, feat[1], positions
                ) * taps_sum(vx, LEAD + first, rows, feat[2], positions)
                query = taps_sum(qx, LEAD + first, rows, feat[0], positions)
                result = query * taps_sum(gx, 8 + first, rows, inner, positions)
                mixed[pl.ds(pl.multiple_of(base + first, TILE), rows), lanes] = result.astype(
                    mixed.dtype
                )

            if not masked:
                for t in range(tiles):
                    tile_of(t * TILE, TILE, False)
                return carry
            for t in range(tiles):
                flag = clean[block * tiles + t]

                @pl.when(flag > 0)
                def _():
                    tile_of(t * TILE, TILE, False)

                @pl.when(flag == 0)
                def _():
                    tile_of(t * TILE, TILE, True)

            return carry

        whole_clean = lead_clean[block]
        for t in range(tiles):
            whole_clean = whole_clean * clean[block * tiles + t]

        @pl.when(whole_clean > 0)
        def _():
            lax.fori_loop(0, channels // LANES, functools.partial(one_chunk, False), 0)

        @pl.when(whole_clean == 0)
        def _():
            lax.fori_loop(0, channels // LANES, functools.partial(one_chunk, True), 0)

    @pl.when(slot == slots - 1)
    def _():
        w_copy.wait()
        step = min(width, 1024)
        for j in range(parts):
            first = lax.rem(core[0] + j, parts) * width if len(outs) > 1 else j * width

            def columns(n, carry):
                at = pl.multiple_of(first + n * step, step)
                part = jnp.dot(
                    mixed[...], w_ref[:, pl.ds(at, step)], preferred_element_type=jnp.float32
                ).astype(jnp.bfloat16)
                to = pl.ds(pl.multiple_of(n * step, step), step)
                if len(outs) > 1:
                    for s in range(slots):
                        outs[j][s, :, to] = part[s * block_rows : (s + 1) * block_rows]
                else:
                    outs[0][j, :, to] = part
                return carry

            lax.fori_loop(0, width // step, columns, 0)


def mix_blocks(scalars, streams, tails, positions, feat_filter, inner_filter, out_weight, parts, block_rows, after):
    slots = scalars[0].shape[0]
    rows, channels = streams[0].shape
    width = out_weight.shape[1] // parts
    lead_per_block = block_rows // LEAD

    def here(s, block_of, *_):
        return (jnp.maximum(block_of[s], 0), 0)

    def before(s, block_of, *_):
        return (jnp.maximum(block_of[s] * lead_per_block - 1, 0), 0)

    whole = lambda shape: pl.BlockSpec(shape, lambda *_: (0,) * len(shape))
    pair = parts == 2
    if pair:
        shapes = [jax.ShapeDtypeStruct((slots, block_rows, width), jnp.bfloat16)] * 2
    else:
        shapes = [jax.ShapeDtypeStruct((parts, slots * block_rows, width), jnp.bfloat16)]
    filled_flops = 2 * slots * block_rows * channels * out_weight.shape[1]
    return pl.pallas_call(
        functools.partial(mix_kernel, slots, parts, width, len(after)),
        out_shape=shapes,
        grid_spec=pltpu.PrefetchScalarGridSpec(
            num_scalar_prefetch=4,
            grid=(slots,),
            in_specs=[pl.BlockSpec((block_rows, channels), here)] * 3
            + [pl.BlockSpec((LEAD, channels), before)] * 3
            + [
                whole(tails.shape),
                pl.BlockSpec((block_rows, LANES), here),
                whole(feat_filter.shape),
                whole(inner_filter.shape),
            ]
            + [pl.BlockSpec(memory_space=pl.ANY)] * (1 + len(after)),
            out_specs=[whole(s.shape) for s in shapes],
            scratch_shapes=[pltpu.VMEM((LEAD + block_rows, LANES), jnp.float32)] * 3
            + [
                pltpu.VMEM((8 + block_rows, LANES), jnp.float32),
                pltpu.VMEM((slots * block_rows, channels), jnp.bfloat16),
                pltpu.VMEM(out_weight.shape, out_weight.dtype),
                pltpu.SemaphoreType.DMA,
            ],
        ),
        compiler_params=pltpu.CompilerParams(
            vmem_limit_bytes=48 * 1024 * 1024, dimension_semantics=("arbitrary",)
        ),
        cost_estimate=pl.CostEstimate(
            flops=filled_flops, bytes_accessed=16 * 1024 * 1024 + slots * 6 * 1024 * 1024, transcendentals=0
        ),
    )(*scalars, *streams, *streams, tails, positions, feat_filter, inner_filter, out_weight, *after)


def unset_kernel(out):
    pass


def unset(shape, dtype):
    return pl.pallas_call(
        unset_kernel,
        out_shape=jax.ShapeDtypeStruct(shape, dtype),
        out_specs=pl.BlockSpec(memory_space=pl.ANY),
        cost_estimate=pl.CostEstimate(flops=0, bytes_accessed=0, transcendentals=0),
    )()


def per_device(
    query_in, key_in, value_in, feat_filter, inner_filter, out_weight, doc_pos, counts, destination
):
    row_count, channels = query_in.shape
    dp_count = lax.axis_size("dp")
    tp_count = lax.axis_size("tensor")
    me = lax.axis_index("dp")
    core = lax.axis_index("tensor").astype(jnp.int32).reshape(1)
    block_count = destination.shape[0]
    block_rows = row_count // block_count
    width = out_weight.shape[1] // tp_count
    streams = (query_in, key_in, value_in)

    tails = lax.ppermute(
        jnp.stack([x[row_count - LEAD :] for x in streams]),
        "dp",
        [(i, i + 1) for i in range(dp_count - 1)],
    )
    positions = jnp.broadcast_to(doc_pos[:, None], (row_count, LANES))
    clean = (jnp.min(doc_pos.reshape(-1, TILE), axis=1) >= TAPS - 1).astype(jnp.int32)
    lead_clean = (doc_pos.reshape(block_count, block_rows)[:, 0] >= 2 * (TAPS - 1)).astype(jnp.int32)

    half = dp_count // 2
    far, near = list(range(half, dp_count)), list(range(1, half)) + [0]
    groups, at = [far[:1]], 0
    for k in range(1, half - 1):
        to = at + (2 if k == 3 else 1)
        groups.append([far[k]] + near[at:to])
        at = to
    groups[-1] += near[at:]
    groups.append(far[half - 1 :])
    order = [r for group in groups for r in group]
    sizes = [len(group) for group in groups]
    partner = jnp.bitwise_xor(me.astype(jnp.int32), jnp.asarray(order, jnp.int32))
    numbers = jnp.arange(block_count, dtype=jnp.int32)
    named = (destination[:, 0][None, :] == partner[:, None]) & (numbers < counts[0])[None, :]
    block_of = jnp.max(jnp.where(named, numbers[None, :], -1), axis=1)

    ready = []
    arrived = []
    result = unset((dp_count, block_rows, width), jnp.bfloat16)
    first = 0
    for group in sizes:
        terms = mix_blocks(
            (block_of[first : first + group], clean, lead_clean, core),
            streams, tails, positions, feat_filter, inner_filter, out_weight, tp_count, block_rows,
            ready[-2] if len(ready) > 1 else [],
        )
        ready.append([])
        arrived.append([])
        if tp_count == 2:
            other = lax.ppermute(terms[1], "tensor", [(0, 1), (1, 0)])
        else:
            summed = lax.psum_scatter(terms[0], "tensor", scatter_dimension=0, tiled=False)
            summed = summed.reshape(group, block_rows, width)
        for s in range(group):
            r = order[first + s]
            if tp_count == 2:
                block = (
                    terms[0][s].astype(jnp.float32) + other[s].astype(jnp.float32)
                ).astype(jnp.bfloat16)
            else:
                block = summed[s]
            ready[-1].append(block)
            if r:
                block = lax.ppermute(block, "dp", [(i, i ^ r) for i in range(dp_count)])
                arrived[-1].append(block)
            result = lax.dynamic_update_index_in_dim(result, block, jnp.bitwise_xor(me, r), 0)
        first += group
    return result.reshape(dp_count * block_rows, width)


def solution(mesh):
    in_specs = (
        P("dp", "tensor"),
        P("dp", "tensor"),
        P("dp", "tensor"),
        P(None, None, "tensor"),
        P(None, "tensor"),
        P("tensor", None),
        P("dp"),
        P("dp"),
        P("dp", None),
    )
    return jax.shard_map(
        per_device, mesh=mesh, in_specs=in_specs, out_specs=P("dp", "tensor"), check_vma=False
    )
```
